32 devices in a mesh: groups: 2 (over x), strip: 16 (over z, y, core).
Axes of the slice: x: 2, y: 2, z: 4, core: 2. Of those that a mesh axis runs over, the one named last changes fastest.
Arguments:
- features: bfloat16 [256, 32, 1024], P(('groups', 'strip')), parts along dimension 0, may hold values from -9 to 9
- valid_rows: int32 [32], P(('groups', 'strip')), parts along dimension 0, may hold values from 1 to 8, as said below
- left_views: int32 [4, 4], P('groups'), parts along dimension 0, may hold values from 0 to 3, each once within a row
- right_step: int32 [4, 4], P('groups'), parts along dimension 0, may hold values from 1 to 3
- offset_tile: int32 [4, 4], P('groups'), parts along dimension 0, may hold values from 0 to 3
Outputs:
- disparity: float32 [2, 256, 1024], P(None, ('groups', 'strip')), parts along dimension 1
The draws below stay inside these ranges and needn't reach their ends.
There are 2 independent parts, one for each index of `groups`. The reference program is written for one: setup_inputs(seed, part) draws one part's arguments, and reference() takes and returns one part's arrays. A program takes and returns all parts, laid end to end along the dimension named above; each array names one. Nothing has to cross between parts.
Inputs may be any that keep to these rules, and one draw needn't show every extreme that they name: `valid_rows`: at least one strip is full in every draw.
All inputs are finite; a program needn't handle non-finite values.
Results may differ from the reference program's by a relative error of at most 0.00075.
Values may be sent and summed in bfloat16 or wider, within the bound.
No kernel may reach another device: no remote copies, remote signals or barrier semaphores. Data moves between devices by JAX's collectives and lax.ppermute only.
A program may use at most 128 MiB of HBM per device.

```python
import jax
import jax.numpy as jnp
from jax import lax

C = 32
LEVELS = 256
BX = 128
TILES = 4
VIEWS = 4
ROUNDS = 2
ROWS_DEV = 8
WIDTH = 1024
HEIGHT = 32
ROWS = 128
STRIPS = 16


def draw_features(key, part):
    key = jax.random.fold_in(key, 11)
    key_base, key_scale = jax.random.split(key, 2)
    channel_scale = jnp.exp(jax.random.uniform(key_scale, (1, C, 1), jnp.float32, -0.7, 0.7))
    base_draw = jax.random.normal(key_base, (ROWS, C, WIDTH), jnp.float32)
    values = base_draw * channel_scale
    return jnp.clip(values, -9.0, 9.0).astype(jnp.bfloat16)


def draw_valid_rows(key, part):
    key = jax.random.fold_in(key, 23)
    key_counts, key_full = jax.random.split(key)
    counts = jax.random.randint(key_counts, (STRIPS,), (ROWS_DEV + 1) // 2, ROWS_DEV + 1)
    full_strip = jax.random.randint(key_full, (), 0, STRIPS)
    return jnp.where(jnp.arange(STRIPS) == full_strip, ROWS_DEV, counts).astype(jnp.int32)


def place_ends(array, own_key, smallest, high):
    longest = array.shape.index(max(array.shape))
    spots = []
    for shift in (0, 1):
        where = [jax.random.randint(jax.random.fold_in(own_key, axis), (), 0, length) for axis, length in enumerate(array.shape)]
        where[longest] = (where[longest] + shift) % array.shape[longest]
        spots.append(tuple(where))
    return array.at[spots[0]].set(smallest).at[spots[1]].set(high)


def setup_inputs(seed: int = 0, part: int = 0) -> dict:
    key_of = jax.random.split(jax.random.key(seed), 6)
    part_splits = jax.random.split(jax.random.fold_in(key_of[5], part), 6)
    features = draw_features(jax.random.fold_in(jax.random.fold_in(key_of[5], part), 71), part)
    valid_rows = draw_valid_rows(jax.random.fold_in(jax.random.fold_in(key_of[5], part), 71), part)
    left_views = jax.vmap(lambda own: jax.random.permutation(own, VIEWS))(jax.random.split(part_splits[2], ROUNDS)).reshape((ROUNDS, VIEWS)).astype(jnp.int32)
    right_step = place_ends(jax.random.randint(part_splits[3], (ROUNDS, VIEWS), 1, VIEWS), jax.random.fold_in(part_splits[3], 1), 1, VIEWS - 1).astype(jnp.int32)
    offset_tile = place_ends(jax.random.randint(part_splits[4], (ROUNDS, VIEWS), 0, TILES), jax.random.fold_in(part_splits[4], 1), 0, TILES - 1).astype(jnp.int32)
    return dict(features=features, valid_rows=valid_rows, left_views=left_views, right_step=right_step, offset_tile=offset_tile)


score_scale = 0.35


def right_windows(right_strip, tile_index):
    height, channels, columns = right_strip.shape
    block_count = columns // BX
    spans = right_strip.reshape(height, channels, block_count, BX)
    leading = jnp.zeros((height, channels, LEVELS // BX + TILES - 1, BX), right_strip.dtype)
    padded = jnp.concatenate([leading, spans], axis=2)
    pieces = []
    for window_part in range((BX + LEVELS) // BX):
        start = (TILES - 1 - tile_index + window_part).astype(jnp.int32)
        pieces.append(lax.dynamic_slice_in_dim(padded, start, block_count, 2))
    return jnp.concatenate(pieces, axis=3)


def regress(padded, tile_index):
    aggregated = 0.25 * padded[:-2] + 0.5 * padded[1:-1] + 0.25 * padded[2:]
    columns = lax.broadcasted_iota(jnp.int32, (BX, BX + LEVELS), 0)
    window_cols = lax.broadcasted_iota(jnp.int32, (BX, BX + LEVELS), 1)
    levels_at = columns + LEVELS - window_cols
    in_band = (levels_at >= 0) & (levels_at < LEVELS)
    logits = jnp.where(in_band, aggregated, jnp.float32(-1e30))
    largest = jnp.max(logits, axis=-1, keepdims=True)
    weights = jnp.where(in_band, jnp.exp(logits - largest), jnp.float32(0.0))
    values = (tile_index * BX + levels_at).astype(jnp.float32)
    return jnp.sum(weights * values, axis=-1) / jnp.sum(weights, axis=-1)


def pair_disparity(left_strip, right_strip, tile_index):
    block_count = WIDTH // BX
    left_blocks = jnp.transpose(left_strip.reshape(HEIGHT, C, block_count, BX), (2, 0, 1, 3))
    windows = jnp.transpose(right_windows(right_strip, tile_index), (2, 0, 1, 3))

    def one_block(operands):
        left_block, right_window = operands
        scores = jnp.einsum("ycx,ycj->yxj", left_block.astype(jnp.float32), right_window.astype(jnp.float32), precision=lax.Precision.HIGHEST) * score_scale
        zero_row = jnp.zeros((1,) + scores.shape[1:], jnp.float32)
        return regress(jnp.concatenate([zero_row, scores, zero_row], 0), tile_index)

    result = lax.map(one_block, (left_blocks, windows))
    return jnp.transpose(result, (1, 0, 2)).reshape(HEIGHT, WIDTH)


def reference(features, valid_rows, left_views, right_step, offset_tile):
    row_ids = jnp.arange(ROWS, dtype=jnp.int32)
    keep_row = (row_ids % ROWS_DEV) >= ROWS_DEV - valid_rows[row_ids // ROWS_DEV]
    masked = jnp.where(keep_row[:, None, None], features, jnp.zeros_like(features))
    rotated = jnp.roll(masked, -(HEIGHT // 2), axis=0)
    by_view = rotated.reshape(VIEWS, HEIGHT, C, WIDTH)
    outputs = []
    for round_index in range(ROUNDS):
        pair_out = []
        for pair_slot in range(VIEWS):
            left_view = left_views[round_index, pair_slot]
            right_view = (left_view + right_step[round_index, pair_slot]) % VIEWS
            tile_index = offset_tile[round_index, pair_slot]
            pair_out.append(pair_disparity(by_view[left_view], by_view[right_view], tile_index))
        outputs.append(jnp.concatenate(pair_out, 0))
    return jnp.roll(jnp.stack(outputs, 0), HEIGHT // 2, axis=1)
```

```python
import math

import jax
import jax.numpy as jnp
from jax import lax
from jax.experimental import pallas as pl
from jax.experimental.pallas import tpu as pltpu
from jax.sharding import PartitionSpec as P

LEVELS = 256
BX = 128
TILES = 4
VIEWS = 4
ROUNDS = 2
PAIRS = ROUNDS * VIEWS
PAD = (TILES - 1) * BX + LEVELS
SCALE = 0.35 * math.log2(math.e)
CHUNKS = (8,)


def slot_of(view, unit):
    return 2 - view if (unit % 2 and view % 2 == 0) else view


def swap_bits(i):
    return ((i & 1) << 1) | (i >> 1)


def tables(strips):
    per_view = strips // VIEWS

    def device(view, unit, core):
        return (view * per_view + 2 * unit + core + per_view // 2) % strips

    units = per_view // 2
    share = []
    for m in range(VIEWS):
        pairs = []
        for unit in range(units):
            order = sorted(range(VIEWS), key=lambda v: slot_of(v, unit))
            for view in range(VIEWS):
                for core in range(2):
                    part = swap_bits(slot_of(view, unit)) ^ m
                    place = 4 * core + part
                    pairs.append((device(view, unit, core), device(order[place // 2], unit, place % 2)))
        share.append(pairs)
    line = []
    for unit in range(units):
        order = sorted(range(VIEWS), key=lambda v: slot_of(v, unit))
        for place in range(8):
            line.append(device(order[place // 2], unit, place % 2))
    down = list(zip(line[:-1], line[1:]))
    return share, down


def regress(scores, half, x_less_b):
    groups = BX // 8

    def part(span, a):
        first = span * BX + 8 * a
        return scores[first : first + 8, half * BX : (half + 1) * BX]

    held = [jnp.where(x_less_b < 8 * a, part(0, a), part(2, a)) for a in range(groups)]
    held += [part(1, a) for a in range(groups)]
    tops = held[:4]
    for i in range(4, 2 * groups):
        tops[i % 4] = jnp.maximum(tops[i % 4], held[i])
    top = jnp.maximum(jnp.maximum(tops[0], tops[1]), jnp.maximum(tops[2], tops[3]))
    top = jnp.broadcast_to(jnp.max(top, axis=0, keepdims=True), (8, BX))
    weights = [jnp.exp2(v - top) for v in held]
    near = weights[groups - 1]
    near_moment = near
    wrapped = jnp.where(x_less_b < 8 * (groups - 1), near, 0.0)
    far = weights[2 * groups - 1]
    far_moment = far
    for a in range(groups - 2, -1, -1):
        near = near + weights[a]
        far = far + weights[groups + a]
        wrapped = jnp.where(x_less_b < 8 * a, near, wrapped)
        if a:
            near_moment = near_moment + near
            far_moment = far_moment + far
    total = near + far
    moment = (
        x_less_b.astype(jnp.float32) * total
        - 8.0 * (near_moment + far_moment)
        + 128.0 * far
        + 256.0 * wrapped
    )
    return jnp.sum(moment, axis=0, keepdims=True) / jnp.sum(total, axis=0, keepdims=True)


def band(numbers, base, above, below, first_block):
    chunks = len(base)
    widths = [a.shape[-1] for a in above]
    channels = above[0].shape[1]
    depth = 4 * channels
    columns = sum(widths)
    count = widths[-1] // BX

    def body(numbers, *refs):
        refs = list(refs)
        base = [[refs.pop(0) for _ in range(VIEWS)] for _ in range(chunks)]
        above = [refs.pop(0) for _ in range(chunks)]
        below = [refs.pop(0) for _ in range(chunks)]
        outs = [refs.pop(0) for _ in range(VIEWS)]
        right, left = refs

        place = numbers[3 * PAIRS]
        unit = place // 8
        bits = place % 4

        def order_of(unit, rank):
            return jnp.where((unit % 2 == 1) & (rank % 2 == 0), 2 - rank, rank)

        def swap(i):
            return (i % 2) * 2 + i // 2

        def view_of(m):
            return order_of(unit, swap(bits ^ m))

        def buffer_of(view, place):
            return (place % 4) ^ swap(order_of(place // 8, view))

        before = jnp.maximum(place - 1, 0)
        after = place + 1
        for m in range(VIEWS):
            view = view_of(m)
            right[m, :PAD, :] = jnp.zeros((PAD, 2 * depth), jnp.bfloat16)
            head, tail = buffer_of(view, before), buffer_of(view, after)
            column = 0
            for c in range(chunks):
                for n in range(widths[c] // BX):
                    span = slice(n * BX, (n + 1) * BX)
                    rows = jnp.concatenate(
                        [above[c][head, :, span], base[c][m][0, :, span], base[c][m][1, :, span], below[c][tail, :, span]],
                        0,
                    )
                    turned = rows.T
                    right[m, PAD + column : PAD + column + BX, :depth] = turned
                    right[m, PAD + column : PAD + column + BX, depth:] = turned
                    column += BX
                    if c < chunks - 1:
                        continue
                    scaled = rows.astype(jnp.float32) * SCALE
                    high = scaled.astype(jnp.bfloat16)
                    low = (scaled - high.astype(jnp.float32)).astype(jnp.bfloat16)
                    for i, value in enumerate((high, low)):
                        quarter = value * jnp.bfloat16(0.25)
                        half = value * jnp.bfloat16(0.5)
                        nothing = jnp.zeros((channels, BX), jnp.bfloat16)
                        q = [quarter[k * channels : (k + 1) * channels] for k in range(4)]
                        h = [half[k * channels : (k + 1) * channels] for k in range(4)]
                        at = slice(i * depth, (i + 1) * depth)
                        left[m, n, at, :BX] = jnp.concatenate([q[0], h[1], q[2], nothing], 0)
                        left[m, n, at, BX:] = jnp.concatenate([nothing, q[1], h[2], q[3]], 0)
        x_less_b = lax.broadcasted_iota(jnp.int32, (8, BX), 1) - lax.broadcasted_iota(jnp.int32, (8, BX), 0)

        for m in range(VIEWS):
            view = view_of(m)

            def one_round(q, carry):
                left_view = numbers[q * VIEWS + view]
                right_view = (left_view + numbers[PAIRS + q * VIEWS + view]) % VIEWS
                tile = numbers[2 * PAIRS + q * VIEWS + view]
                a, b = buffer_of(left_view, place), buffer_of(right_view, place)
                shift = (tile * BX).astype(jnp.float32)
                for n in range(count):
                    start = pl.multiple_of((TILES - 1 + first_block + n - tile) * BX, BX)
                    scores = jnp.dot(
                        right[b, pl.ds(start, BX + LEVELS), :], left[a, n], preferred_element_type=jnp.float32
                    )
                    for r in range(2):
                        outs[m][q, r : r + 1, n * BX : (n + 1) * BX] = regress(scores, r, x_less_b) + shift
                return carry

            lax.fori_loop(0, ROUNDS, one_round, 0)

    vmem = pl.BlockSpec(memory_space=pltpu.VMEM)
    operands = [b for chunk in base for b in chunk] + list(above) + list(below)
    return pl.pallas_call(
        body,
        out_shape=[jax.ShapeDtypeStruct((ROUNDS, 2, widths[-1]), jnp.float32)] * VIEWS,
        in_specs=[pl.BlockSpec(memory_space=pltpu.SMEM)] + [vmem] * len(operands),
        out_specs=[vmem] * VIEWS,
        scratch_shapes=[
            pltpu.VMEM((VIEWS, PAD + columns, 2 * depth), jnp.bfloat16),
            pltpu.VMEM((VIEWS, count, 2 * depth, 2 * BX), jnp.bfloat16),
        ],
        compiler_params=pltpu.CompilerParams(vmem_limit_bytes=48 << 20),
        name="band",
    )(numbers, *operands)


def per_device(features, valid_rows, left_views, right_step, offset_tile):
    row_count, _, col_count = features.shape
    strips = lax.axis_size("strip")
    per_view = strips // VIEWS
    share, down = tables(strips)
    index = (lax.axis_index("strip") - per_view // 2) % strips
    view, spot = index // per_view, index % per_view
    unit, core = spot // 2, spot % 2
    slot = jnp.where((unit % 2 == 1) & (view % 2 == 0), 2 - view, view)
    first = (slot % 2) * 2 + slot // 2
    place = 8 * unit + 2 * slot + core
    numbers = jnp.concatenate(
        [left_views.reshape(-1), right_step.reshape(-1), offset_tile.reshape(-1), place.astype(jnp.int32).reshape(1)]
    )
    row_ids = lax.broadcasted_iota(jnp.int32, (row_count, 1, 1), 0)
    masked = jnp.where(row_ids >= row_count - valid_rows[0], features, jnp.zeros_like(features))
    bounds = [0]
    for blocks in CHUNKS:
        bounds.append(bounds[-1] + blocks * BX)
    base, above, below, results = [], [], [], []
    for c in range(len(CHUNKS)):
        got = []
        for m in range(VIEWS):
            piece = lax.dynamic_slice_in_dim(masked, 2 * (first ^ m), 2, 0)[:, :, bounds[c] : bounds[c + 1]]
            got.append(lax.ppermute(piece, "strip", share[m]))
        base.append(got)
    for c in range(len(CHUNKS)):
        heads = jnp.concatenate([g[:1] for g in base[c]], 0)
        tails = jnp.concatenate([g[1:] for g in base[c]], 0)
        above.append(lax.ppermute(tails, "strip", down))
        below.append(lax.ppermute(heads, "strip", [(j, i) for i, j in down]))
    for c in range(len(CHUNKS)):
        sent = band(numbers, base[: c + 1], above[: c + 1], below[: c + 1], bounds[c] // BX)
        back = [lax.ppermute(sent[m], "strip", [(j, i) for i, j in share[m]]) for m in range(VIEWS)]
        odd = first % 2 == 1
        high = first // 2 == 1
        back = [jnp.where(odd, back[m ^ 1], back[m]) for m in range(VIEWS)]
        back = [jnp.where(high, back[m ^ 2], back[m]) for m in range(VIEWS)]
        results.append(jnp.concatenate(back, 1))
    return jnp.concatenate(results, 2)


def solution(mesh):
    return jax.shard_map(
        per_device,
        mesh=mesh,
        in_specs=(
            P(("groups", "strip"), None, None),
            P(("groups", "strip")),
            P("groups", None),
            P("groups", None),
            P("groups", None),
        ),
        out_specs=P(None, ("groups", "strip"), None),
        check_vma=False,
    )
```

```python
import math

import jax
import jax.numpy as jnp
from jax import lax
from jax.experimental import pallas as pl
from jax.experimental.pallas import tpu as pltpu
from jax.sharding import PartitionSpec as P

LEVELS = 256
BX = 128
TILES = 4
VIEWS = 4
ROUNDS = 2
PAIRS = ROUNDS * VIEWS
FLIP = 3
PAD = (TILES - 1) * BX + LEVELS
SCALE = 0.35 * math.log2(math.e)


def slot_of(view, unit):
    return 2 - view if (unit % 2 and view % 2 == 0) else view


def swap_bits(i):
    return ((i & 1) << 1) | (i >> 1)


def tables(strips):
    per_view = strips // VIEWS

    def device(view, unit, core):
        return (view * per_view + 2 * unit + core + per_view // 2) % strips

    units = per_view // 2
    share = []
    for m in range(VIEWS):
        pairs = []
        for unit in range(units):
            order = sorted(range(VIEWS), key=lambda v: slot_of(v, unit))
            for view in range(VIEWS):
                for core in range(2):
                    part = swap_bits(slot_of(view, unit)) ^ m ^ FLIP
                    place = 4 * core + part
                    pairs.append((device(view, unit, core), device(order[place // 2], unit, place % 2)))
        share.append(pairs)
    line = []
    for unit in range(units):
        order = sorted(range(VIEWS), key=lambda v: slot_of(v, unit))
        for place in range(8):
            line.append(device(order[place // 2], unit, place % 2))
    inner = [(line[i], line[i ^ 1]) for i in range(len(line))]
    outer = [(line[i], line[i + 1]) for i in range(1, len(line) - 1, 2)]
    return share, inner, outer + [(j, i) for i, j in outer]


def regress(scores, half, x_less_b):
    groups = BX // 8

    def part(span, a):
        first = (span + half) * BX + 8 * a
        return scores[first : first + 8, half * BX : (half + 1) * BX]

    held = [jnp.where(x_less_b < 8 * a, part(0, a), part(2, a)) for a in range(groups)]
    held += [part(1, a) for a in range(groups)]
    tops = held[:4]
    for i in range(4, 2 * groups):
        tops[i % 4] = jnp.maximum(tops[i % 4], held[i])
    top = jnp.maximum(jnp.maximum(tops[0], tops[1]), jnp.maximum(tops[2], tops[3]))
    top = jnp.broadcast_to(jnp.max(top, axis=0, keepdims=True), (8, BX))
    weights = [jnp.exp2((v - top) * SCALE) for v in held]
    near = weights[groups - 1]
    near_moment = near
    wrapped = jnp.where(x_less_b < 8 * (groups - 1), near, 0.0)
    far = weights[2 * groups - 1]
    far_moment = far
    for a in range(groups - 2, -1, -1):
        near = near + weights[a]
        far = far + weights[groups + a]
        wrapped = jnp.where(x_less_b < 8 * a, near, wrapped)
        if a:
            near_moment = near_moment + near
            far_moment = far_moment + far
    total = near + far
    moment = (
        x_less_b.astype(jnp.float32) * total
        - 8.0 * (near_moment + far_moment)
        + 128.0 * far
        + 256.0 * wrapped
    )
    return jnp.sum(moment, axis=0, keepdims=True) / jnp.sum(total, axis=0, keepdims=True)


def band(numbers, base, rim, done):
    inner = done is None
    _, channels, columns = base[0].shape
    depth = 4 * channels

    def body(numbers, *refs):
        base, rim = refs[:VIEWS], refs[VIEWS]
        if inner:
            result, right, left = refs[VIEWS + 1 :]
        else:
            done = refs[VIEWS + 1]
            outs = refs[VIEWS + 2 : 2 * VIEWS + 2]
            right, left, result = refs[2 * VIEWS + 2 :]

        place = numbers[3 * PAIRS]
        core = place % 2

        def order_of(unit, rank):
            return jnp.where((unit % 2 == 1) & (rank % 2 == 0), 2 - rank, rank)

        def swap(i):
            return (i % 2) * 2 + i // 2

        def view_of(m):
            return order_of(place // 8, swap((place % 4) ^ m ^ FLIP))

        def buffer_of(view, place):
            return (place % 4) ^ swap(order_of(place // 8, view)) ^ FLIP

        sender = place + 1 - 2 * core if inner else jnp.maximum(place - 1 + 2 * core, 0)
        middle = 1 - core if inner else core
        heavy = 0.25 + 0.25 * middle.astype(jnp.float32)
        shares = [jnp.full((channels, BX), w).astype(jnp.bfloat16) for w in (0.75 - heavy, heavy, 0.25)]
        nothing = jnp.zeros((channels, BX), jnp.bfloat16)
        for m in range(VIEWS):
            there = buffer_of(view_of(m), sender)
            right[m, :PAD, :] = jnp.zeros((PAD, depth), jnp.bfloat16)
            for n in range(columns // BX):
                span = slice(n * BX, (n + 1) * BX)
                rows = [base[m][0, :, span], base[m][1, :, span], rim[there, :, span]]
                right[m, PAD + n * BX : PAD + (n + 1) * BX, :] = jnp.concatenate(rows + [nothing], 0).T
                left[m, :, span] = jnp.concatenate([r * w for r, w in zip(rows, shares)] + [nothing], 0)
        x_less_b = lax.broadcasted_iota(jnp.int32, (8, BX), 1) - lax.broadcasted_iota(jnp.int32, (8, BX), 0)

        def one_pair(j, carry):
            view = j % VIEWS
            left_view = numbers[j]
            right_view = (left_view + numbers[PAIRS + j]) % VIEWS
            tile = numbers[2 * PAIRS + j]
            a, b = buffer_of(left_view, place), buffer_of(right_view, place)
            shift = (tile * BX).astype(jnp.float32)
            home = ROUNDS * buffer_of(view, place) + j // VIEWS
            for n in range(0, columns // BX, 2):
                start = pl.multiple_of((TILES - 1 + n - tile) * BX, BX)
                scores = jnp.dot(
                    right[b, pl.ds(start, 2 * BX + LEVELS), :],
                    left[a, :, n * BX : (n + 2) * BX],
                    preferred_element_type=jnp.float32,
                )
                for i in range(2):
                    result[home, :, (n + i) * BX : (n + i + 1) * BX] = regress(scores, i, x_less_b) + shift
            return carry

        lax.fori_loop(0, PAIRS, one_pair, 0, unroll=4)
        if not inner:
            for m in range(VIEWS):
                for q in range(ROUNDS):
                    both = [done[ROUNDS * m + q], result[ROUNDS * m + q]]
                    outs[m][q, 0:1, :] = jnp.where(core == 0, both[1], both[0])
                    outs[m][q, 1:2, :] = jnp.where(core == 0, both[0], both[1])

    vmem = pl.BlockSpec(memory_space=pltpu.VMEM)
    operands = list(base) + [rim] + ([] if inner else [done])
    every = jax.ShapeDtypeStruct((PAIRS, 1, columns), jnp.float32)
    scratch = [pltpu.VMEM((VIEWS, PAD + columns, depth), jnp.bfloat16), pltpu.VMEM((VIEWS, depth, columns), jnp.bfloat16)]
    return pl.pallas_call(
        body,
        out_shape=every if inner else [jax.ShapeDtypeStruct((ROUNDS, 2, columns), jnp.float32)] * VIEWS,
        in_specs=[pl.BlockSpec(memory_space=pltpu.SMEM)] + [vmem] * len(operands),
        out_specs=vmem if inner else [vmem] * VIEWS,
        scratch_shapes=scratch if inner else scratch + [pltpu.VMEM(every.shape, every.dtype)],
        compiler_params=pltpu.CompilerParams(vmem_limit_bytes=48 << 20),
        name="band_inner" if inner else "band_outer",
    )(numbers, *operands)


def per_device(features, valid_rows, left_views, right_step, offset_tile):
    row_count = features.shape[0]
    strips = lax.axis_size("strip")
    per_view = strips // VIEWS
    share, siblings, neighbours = tables(strips)
    index = (lax.axis_index("strip") - per_view // 2) % strips
    view, spot = index // per_view, index % per_view
    unit, core = spot // 2, spot % 2
    slot = jnp.where((unit % 2 == 1) & (view % 2 == 0), 2 - view, view)
    first = ((slot % 2) * 2 + slot // 2) ^ FLIP
    place = 8 * unit + 2 * slot + core
    numbers = jnp.concatenate(
        [left_views.reshape(-1), right_step.reshape(-1), offset_tile.reshape(-1), place.astype(jnp.int32).reshape(1)]
    )
    row_ids = lax.broadcasted_iota(jnp.int32, (row_count, 1, 1), 0)
    masked = jnp.where(row_ids >= row_count - valid_rows[0], features, jnp.zeros_like(features))
    base = []
    for m in range(VIEWS):
        base.append(lax.ppermute(lax.dynamic_slice_in_dim(masked, 2 * (first ^ m), 2, 0), "strip", share[m]))
    numbers, base = lax.optimization_barrier((numbers, base))
    rows = [jnp.concatenate([lax.dynamic_slice_in_dim(g, r, 1, 0) for g in base], 0) for r in (1 - core, core)]
    beside = lax.ppermute(rows[0], "strip", siblings)
    beyond = lax.ppermute(rows[1], "strip", neighbours)
    sent = band(numbers, base, beyond, band(numbers, base, beside, None))
    back = [lax.ppermute(sent[m], "strip", [(j, i) for i, j in share[m]]) for m in range(VIEWS)]
    back = [jnp.where(first % 2 == 1, back[m ^ 1], back[m]) for m in range(VIEWS)]
    back = [jnp.where(first // 2 == 1, back[m ^ 2], back[m]) for m in range(VIEWS)]
    return jnp.concatenate(back, 1)


def solution(mesh):
    return jax.shard_map(
        per_device,
        mesh=mesh,
        in_specs=(
            P(("groups", "strip"), None, None),
            P(("groups", "strip")),
            P("groups", None),
            P("groups", None),
            P("groups", None),
        ),
        out_specs=P(None, ("groups", "strip"), None),
        check_vma=False,
    )
```

```python
import math

import jax
import jax.numpy as jnp
from jax import lax
from jax.experimental import pallas as pl
from jax.experimental.pallas import tpu as pltpu
from jax.sharding import PartitionSpec as P

LEVELS = 256
BX = 128
TILES = 4
VIEWS = 4
ROUNDS = 2
PAIRS = ROUNDS * VIEWS
PAD = (TILES - 1) * BX + LEVELS
SCALE = 0.35 * math.log2(math.e)


def slot_of(view, unit):
    return (view + 1) % VIEWS if unit % 2 else VIEWS - 1 - view


def swap_bits(i):
    return ((i & 1) << 1) | (i >> 1)


def tables(strips):
    per_view = strips // VIEWS

    def device(view, unit, core):
        return (view * per_view + 2 * unit + core + per_view // 2) % strips

    units = per_view // 2
    share = []
    for m in range(VIEWS):
        pairs = []
        for unit in range(units):
            order = sorted(range(VIEWS), key=lambda v: slot_of(v, unit))
            for view in range(VIEWS):
                for core in range(2):
                    part = swap_bits(slot_of(view, unit)) ^ m
                    place = 4 * core + part
                    pairs.append((device(view, unit, core), device(order[place // 2], unit, place % 2)))
        share.append(pairs)
    line = []
    for unit in range(units):
        order = sorted(range(VIEWS), key=lambda v: slot_of(v, unit))
        for place in range(8):
            line.append(device(order[place // 2], unit, place % 2))
    inner = [(line[i], line[i ^ 1]) for i in range(len(line))]
    outer = [(line[i], line[i + 1]) for i in range(1, len(line) - 1, 2)]
    home = []
    for e in range(2):
        pairs = []
        for unit in range(units):
            order = sorted(range(VIEWS), key=lambda v: slot_of(v, unit))
            for view in range(VIEWS):
                for core in range(2):
                    slot = slot_of(view, unit)
                    sender = device(order[2 * core + (slot % 2 ^ e ^ 1)], unit, slot // 2)
                    pairs.append((sender, device(view, unit, core)))
        home.append(pairs)
    return share, inner, outer + [(j, i) for i, j in outer], home


def regress(scores, half, x_less_b):
    groups = BX // 8

    def part(span, a):
        first = (span + half) * BX + 8 * a
        return scores[first : first + 8, half * BX : (half + 1) * BX]

    held = [jnp.where(x_less_b < 8 * a, part(0, a), part(2, a)) for a in range(groups)]
    held += [part(1, a) for a in range(groups)]
    tops = held[:4]
    for i in range(4, 2 * groups):
        tops[i % 4] = jnp.maximum(tops[i % 4], held[i])
    top = jnp.maximum(jnp.maximum(tops[0], tops[1]), jnp.maximum(tops[2], tops[3]))
    top = jnp.broadcast_to(jnp.max(top, axis=0, keepdims=True), (8, BX))
    weights = [jnp.exp2((v - top) * SCALE) for v in held]
    near = weights[groups - 1]
    near_moment = near
    wrapped = jnp.where(x_less_b < 8 * (groups - 1), near, 0.0)
    far = weights[2 * groups - 1]
    far_moment = far
    for a in range(groups - 2, -1, -1):
        near = near + weights[a]
        far = far + weights[groups + a]
        wrapped = jnp.where(x_less_b < 8 * a, near, wrapped)
        if a:
            near_moment = near_moment + near
            far_moment = far_moment + far
    total = near + far
    moment = (
        x_less_b.astype(jnp.float32) * total
        - 8.0 * (near_moment + far_moment)
        + 128.0 * far
        + 256.0 * wrapped
    )
    return jnp.sum(moment, axis=0, keepdims=True) / jnp.sum(total, axis=0, keepdims=True)


def band(numbers, base, rim, done):
    inner = done is None
    _, channels, columns = base[0].shape
    depth = 4 * channels

    def body(numbers, *refs):
        base, rim = refs[:VIEWS], refs[VIEWS]
        if inner:
            result, right, left = refs[VIEWS + 1 :]
        else:
            done = refs[VIEWS + 1]
            outs = refs[VIEWS + 2 : VIEWS + 4]
            right, left, result = refs[VIEWS + 4 :]

        place = numbers[3 * PAIRS]
        core = place % 2

        def slot_in(unit, view):
            return jnp.where(unit % 2 == 1, (view + 1) % VIEWS, VIEWS - 1 - view)

        def swap(i):
            return (i % 2) * 2 + i // 2

        def view_of(m):
            slot = swap((place % 4) ^ m)
            return jnp.where(place // 8 % 2 == 1, (slot + VIEWS - 1) % VIEWS, VIEWS - 1 - slot)

        def buffer_of(view, place):
            return (place % 4) ^ swap(slot_in(place // 8, view))

        sender = place + 1 - 2 * core if inner else jnp.maximum(place - 1 + 2 * core, 0)
        middle = 1 - core if inner else core
        heavy = 0.25 + 0.25 * middle.astype(jnp.float32)
        shares = [jnp.full((channels, BX), w).astype(jnp.bfloat16) for w in (0.75 - heavy, heavy, 0.25)]
        nothing = jnp.zeros((channels, BX), jnp.bfloat16)
        for m in range(VIEWS):
            there = buffer_of(view_of(m), sender)
            right[m, :PAD, :] = jnp.zeros((PAD, depth), jnp.bfloat16)
            for n in range(columns // BX):
                span = slice(n * BX, (n + 1) * BX)
                rows = [base[m][0, :, span], base[m][1, :, span], rim[there, :, span]]
                right[m, PAD + n * BX : PAD + (n + 1) * BX, :] = jnp.concatenate(rows + [nothing], 0).T
                left[m, :, span] = jnp.concatenate([r * w for r, w in zip(rows, shares)] + [nothing], 0)
        x_less_b = lax.broadcasted_iota(jnp.int32, (8, BX), 1) - lax.broadcasted_iota(jnp.int32, (8, BX), 0)

        def one_pair(j, carry):
            view = j % VIEWS
            left_view = numbers[j]
            right_view = (left_view + numbers[PAIRS + j]) % VIEWS
            tile = numbers[2 * PAIRS + j]
            a, b = buffer_of(left_view, place), buffer_of(right_view, place)
            shift = (tile * BX).astype(jnp.float32)
            there = slot_in(place // 8, view)
            home = ROUNDS * (2 * ((there // 2) ^ core) + (there ^ (place % 8 // 2) ^ 1) % 2) + j // VIEWS
            for n in range(0, columns // BX, 2):
                start = pl.multiple_of((TILES - 1 + n - tile) * BX, BX)
                scores = jnp.dot(
                    right[b, pl.ds(start, 2 * BX + LEVELS), :],
                    left[a, :, n * BX : (n + 2) * BX],
                    preferred_element_type=jnp.float32,
                )
                for i in range(2):
                    result[home, :, (n + i) * BX : (n + i + 1) * BX] = regress(scores, i, x_less_b) + shift
            return carry

        lax.fori_loop(0, PAIRS, one_pair, 0, unroll=4)
        if not inner:
            for i in range(2):
                for e in range(2):
                    for q in range(ROUNDS):
                        at = ROUNDS * (2 * i + e) + q
                        outs[i][e, q, 0:1, :] = jnp.where(core == 0, result[at], done[at])
                        outs[i][e, q, 1:2, :] = jnp.where(core == 0, done[at], result[at])

    vmem = pl.BlockSpec(memory_space=pltpu.VMEM)
    operands = list(base) + [rim] + ([] if inner else [done])
    every = jax.ShapeDtypeStruct((PAIRS, 1, columns), jnp.float32)
    scratch = [pltpu.VMEM((VIEWS, PAD + columns, depth), jnp.bfloat16), pltpu.VMEM((VIEWS, depth, columns), jnp.bfloat16)]
    return pl.pallas_call(
        body,
        out_shape=every if inner else [jax.ShapeDtypeStruct((2, ROUNDS, 2, columns), jnp.float32)] * 2,
        in_specs=[pl.BlockSpec(memory_space=pltpu.SMEM)] + [vmem] * len(operands),
        out_specs=vmem if inner else [vmem] * 2,
        scratch_shapes=scratch if inner else scratch + [pltpu.VMEM(every.shape, every.dtype)],
        compiler_params=pltpu.CompilerParams(vmem_limit_bytes=48 << 20),
        name="band_inner" if inner else "band_outer",
    )(numbers, *operands)


def per_device(features, valid_rows, left_views, right_step, offset_tile):
    row_count = features.shape[0]
    strips = lax.axis_size("strip")
    per_view = strips // VIEWS
    share, siblings, neighbours, home = tables(strips)
    index = (lax.axis_index("strip") - per_view // 2) % strips
    view, spot = index // per_view, index % per_view
    unit, core = spot // 2, spot % 2
    slot = jnp.where(unit % 2 == 1, (view + 1) % VIEWS, VIEWS - 1 - view)
    first = (slot % 2) * 2 + slot // 2
    place = 8 * unit + 2 * slot + core
    numbers = jnp.concatenate(
        [left_views.reshape(-1), right_step.reshape(-1), offset_tile.reshape(-1), place.astype(jnp.int32).reshape(1)]
    )
    row_ids = lax.broadcasted_iota(jnp.int32, (row_count, 1, 1), 0)
    masked = jnp.where(row_ids >= row_count - valid_rows[0], features, jnp.zeros_like(features))
    base = []
    for m in range(VIEWS):
        base.append(lax.ppermute(lax.dynamic_slice_in_dim(masked, 2 * (first ^ m), 2, 0), "strip", share[m]))
    numbers, base = lax.optimization_barrier((numbers, base))
    rows = [jnp.concatenate([lax.dynamic_slice_in_dim(g, r, 1, 0) for g in base], 0) for r in (1 - core, core)]
    beside = lax.ppermute(rows[0], "strip", siblings)
    beyond = lax.ppermute(rows[1], "strip", neighbours)
    kept, given = band(numbers, base, beyond, band(numbers, base, beside, None))
    taken = lax.ppermute(given, "strip", siblings)
    sent = jnp.where(core == 0, jnp.concatenate([kept, taken], 2), jnp.concatenate([taken, kept], 2))
    back = [lax.ppermute(sent[e], "strip", home[e]) for e in range(2)]
    return jnp.where(slot % 2 == 0, jnp.concatenate(back[::-1], 1), jnp.concatenate(back, 1))


def solution(mesh):
    return jax.shard_map(
        per_device,
        mesh=mesh,
        in_specs=(
            P(("groups", "strip"), None, None),
            P(("groups", "strip")),
            P("groups", None),
            P("groups", None),
            P("groups", None),
        ),
        out_specs=P(None, ("groups", "strip"), None),
        check_vma=False,
    )
```

```python
import functools
import math

import jax
import jax.numpy as jnp
from jax import lax
from jax.experimental import pallas as pl
from jax.experimental.pallas import tpu as pltpu
from jax.sharding import PartitionSpec as P

LEVELS = 256
BX = 128
TILES = 4
VIEWS = 4
ROUNDS = 2
PAIRS = ROUNDS * VIEWS
UNROLL = 4
PAD = (TILES - 1) * BX + LEVELS
SCALE = 0.35 * math.log2(math.e)


def slot_of(view, unit):
    return (view + 1) % VIEWS if unit % 2 else VIEWS - 1 - view


def swap_bits(i):
    return ((i & 1) << 1) | (i >> 1)


def tables(strips):
    per_view = strips // VIEWS

    def device(view, unit, core):
        return (view * per_view + 2 * unit + core + per_view // 2) % strips

    units = per_view // 2
    share = []
    for m in range(VIEWS):
        pairs = []
        for unit in range(units):
            order = sorted(range(VIEWS), key=lambda v: slot_of(v, unit))
            for view in range(VIEWS):
                for core in range(2):
                    slot, here = slot_of(view, unit), device(view, unit, core)
                    place = 4 * core + (swap_bits(slot) ^ m)
                    there = device(order[place // 2], unit, place % 2)
                    pairs.append((here, device(order[slot ^ 1], unit, core) if there == here else there))
        share.append(pairs)
    line = []
    for unit in range(units):
        order = sorted(range(VIEWS), key=lambda v: slot_of(v, unit))
        for place in range(8):
            line.append(device(order[place // 2], unit, place % 2))
    inner = [(line[i], line[i ^ 1]) for i in range(len(line))]
    outer = [(line[i], line[(i + 1) % len(line)]) for i in range(1, len(line), 2)]
    home = []
    for e in range(2):
        pairs = []
        for unit in range(units):
            order = sorted(range(VIEWS), key=lambda v: slot_of(v, unit))
            for view in range(VIEWS):
                for core in range(2):
                    slot = slot_of(view, unit)
                    sender, here = device(order[2 * core + (slot % 2 ^ e ^ 1)], unit, slot // 2), device(view, unit, core)
                    pairs.append((device(order[slot ^ 1], unit, core) if sender == here else sender, here))
        home.append(pairs)
    return share, inner, outer + [(j, i) for i, j in outer], home


def regress(scores, half, x_less_b):
    groups = BX // 8

    def part(span, a):
        first = (span + half) * BX + 8 * a
        return scores[first : first + 8, half * BX : (half + 1) * BX]

    near = [jnp.where(x_less_b < 8 * a, part(0, a), part(2, a)) for a in range(groups)]
    far = [part(1, a) for a in range(groups)]
    tops = [functools.reduce(jnp.maximum, near), functools.reduce(jnp.maximum, far)]
    top = jnp.broadcast_to(jnp.max(jnp.maximum(*tops), axis=0, keepdims=True), (8, BX))

    def weight(value):
        return jnp.exp2((value - top) * SCALE)

    total = moment = weight(far[-1])
    for value in far[-2::-1]:
        total = total + weight(value)
        moment = moment + total
    wrapped = total
    for a in range(groups - 1, -1, -1):
        total = total + weight(near[a])
        wrapped = jnp.where(x_less_b < 8 * a, total, wrapped)
        if a:
            moment = moment + total
    moment = x_less_b.astype(jnp.float32) * total - 8.0 * moment + 256.0 * wrapped
    return jnp.sum(moment, axis=0, keepdims=True) / jnp.sum(total, axis=0, keepdims=True)


class Place:
    def __init__(self, place):
        self.place = place
        self.unit, self.slot, self.core = place // 8, place % 8 // 2, place % 2

    def slot_of(self, view):
        return jnp.where(self.unit % 2 == 1, (view + 1) % VIEWS, VIEWS - 1 - view)

    def view_at(self, slot):
        return jnp.where(self.unit % 2 == 1, (slot + VIEWS - 1) % VIEWS, VIEWS - 1 - slot)

    def view_of(self, buffer):
        return self.view_at(swap_bits((self.place % 4) ^ buffer))

    def buffer_of(self, view):
        return (self.place % 4) ^ swap_bits(self.slot_of(view))

    def view_home(self, group, e):
        return self.view_at(2 * (self.core ^ group) + (e ^ 1 ^ (self.slot % 2)))


def correlate(numbers, at, right, left, result, groups):
    columns = result.shape[-1]
    x_less_b = lax.broadcasted_iota(jnp.int32, (8, BX), 1) - lax.broadcasted_iota(jnp.int32, (8, BX), 0)

    def one_pair(i, carry):
        q, e, group = i % 2, i // 2 % 2, i // 4
        j = VIEWS * q + at.view_home(group, e)
        left_view = numbers[j]
        right_view = (left_view + numbers[PAIRS + j]) % VIEWS
        tile = numbers[2 * PAIRS + j]
        a, b = at.buffer_of(left_view), at.buffer_of(right_view)
        shift = (tile * BX).astype(jnp.float32)
        for n in range(0, columns // BX, 2):
            start = pl.multiple_of((TILES - 1 + n - tile) * BX, BX)
            scores = jnp.dot(
                right[b, pl.ds(start, 2 * BX + LEVELS), :],
                left[a, :, n * BX : (n + 2) * BX],
                preferred_element_type=jnp.float32,
            )
            for k in range(2):
                result[i, :, (n + k) * BX : (n + k + 1) * BX] = regress(scores, k, x_less_b) + shift
        return carry

    lax.fori_loop(4 * groups[0], 4 * groups[-1] + 4, one_pair, 0, unroll=UNROLL)


def shares_of(middle, channels):
    heavy = 0.25 + 0.25 * middle.astype(jnp.float32)
    return [jnp.full((channels, BX), w).astype(jnp.bfloat16) for w in (0.75 - heavy, heavy)]


def band_inner(numbers, base, rim):
    _, channels, columns = base[0].shape
    depth = 4 * channels

    def body(numbers, *refs):
        base, (rim, result, right, outer_left, left) = refs[:VIEWS], refs[VIEWS:]
        at = Place(numbers[3 * PAIRS])
        beside = Place(at.place + 1 - 2 * at.core)
        inner, outer = shares_of(1 - at.core, channels), shares_of(at.core, channels)
        nothing = jnp.zeros((channels, BX), jnp.bfloat16)
        for m in range(VIEWS):
            there = beside.buffer_of(at.view_of(m))
            right[m, :PAD, :] = jnp.zeros((PAD, depth), jnp.bfloat16)
            for n in range(columns // BX):
                span = slice(n * BX, (n + 1) * BX)
                pair = [base[m][0, :, span], base[m][1, :, span]]
                third = rim[there, :, span]
                right[m, PAD + n * BX : PAD + (n + 1) * BX, :] = jnp.concatenate([third] + pair + [nothing], 0).T
                mixed = [r * w for r, w in zip(pair, inner)]
                left[m, :, span] = jnp.concatenate([third * jnp.bfloat16(0.25)] + mixed + [nothing], 0)
                mixed = [r * w for r, w in zip(pair, outer)]
                outer_left[m, channels:, span] = jnp.concatenate(mixed + [nothing], 0)
        correlate(numbers, at, right, left, result, (0, 1))

    vmem = pl.BlockSpec(memory_space=pltpu.VMEM)
    return pl.pallas_call(
        body,
        out_shape=[
            jax.ShapeDtypeStruct((PAIRS, 1, columns), jnp.float32),
            jax.ShapeDtypeStruct((VIEWS, PAD + columns, depth), jnp.bfloat16),
            jax.ShapeDtypeStruct((VIEWS, depth, columns), jnp.bfloat16),
        ],
        in_specs=[pl.BlockSpec(memory_space=pltpu.SMEM)] + [vmem] * (VIEWS + 1),
        out_specs=[vmem] * 3,
        scratch_shapes=[pltpu.VMEM((VIEWS, depth, columns), jnp.bfloat16)],
        compiler_params=pltpu.CompilerParams(vmem_limit_bytes=48 << 20),
        name="band_inner",
    )(numbers, *base, rim)


def both_rows(core, first, second, group, out):
    for e in range(2):
        for q in range(ROUNDS):
            i = 4 * group + 2 * e + q
            out[e, q, 0:1, :] = jnp.where(core == 0, first[i], second[i])
            out[e, q, 1:2, :] = jnp.where(core == 0, second[i], first[i])


def band_given(numbers, rim, done, right, left, places):
    _, channels, columns = rim.shape

    def body(numbers, rim, done, right_in, left_in, given, right, left, result):
        at = Place(numbers[3 * PAIRS])
        beyond = Place((at.place - 1 + 2 * at.core + places) % places)
        edge = at.place == jnp.where(at.core == 0, 0, places - 1)
        share = jnp.full((channels, BX), jnp.where(edge, 0.0, 0.25)).astype(jnp.bfloat16)
        for m in range(VIEWS):
            there = beyond.buffer_of(at.view_of(m))
            for n in range(columns // BX):
                span = slice(n * BX, (n + 1) * BX)
                third = rim[there, :, span]
                right[m, PAD + n * BX : PAD + (n + 1) * BX, :channels] = third.T
                left[m, :channels, span] = third * share
        correlate(numbers, at, right, left, result, (1,))
        both_rows(at.core, result, done, 1, given)

    vmem = pl.BlockSpec(memory_space=pltpu.VMEM)
    return pl.pallas_call(
        body,
        out_shape=[
            jax.ShapeDtypeStruct((2, ROUNDS, 2, columns), jnp.float32),
            jax.ShapeDtypeStruct(right.shape, right.dtype),
            jax.ShapeDtypeStruct(left.shape, left.dtype),
        ],
        in_specs=[pl.BlockSpec(memory_space=pltpu.SMEM)] + [vmem] * 4,
        out_specs=[vmem] * 3,
        input_output_aliases={3: 1, 4: 2},
        scratch_shapes=[pltpu.VMEM(done.shape, done.dtype)],
        compiler_params=pltpu.CompilerParams(vmem_limit_bytes=48 << 20),
        name="band_given",
    )(numbers, rim, done, right, left)


def band_kept(numbers, done, right, left):
    columns = done.shape[-1]

    def body(numbers, done, right, left, kept, result):
        at = Place(numbers[3 * PAIRS])
        correlate(numbers, at, right, left, result, (0,))
        both_rows(at.core, result, done, 0, kept)

    vmem = pl.BlockSpec(memory_space=pltpu.VMEM)
    return pl.pallas_call(
        body,
        out_shape=jax.ShapeDtypeStruct((2, ROUNDS, 2, columns), jnp.float32),
        in_specs=[pl.BlockSpec(memory_space=pltpu.SMEM)] + [vmem] * 3,
        out_specs=vmem,
        scratch_shapes=[pltpu.VMEM(done.shape, done.dtype)],
        compiler_params=pltpu.CompilerParams(vmem_limit_bytes=48 << 20),
        name="band_kept",
    )(numbers, done, right, left)


def per_device(features, valid_rows, left_views, right_step, offset_tile):
    row_count = features.shape[0]
    strips = lax.axis_size("strip")
    per_view = strips // VIEWS
    share, siblings, neighbours, home = tables(strips)
    index = (lax.axis_index("strip") - per_view // 2) % strips
    view, spot = index // per_view, index % per_view
    unit, core = spot // 2, spot % 2
    slot = jnp.where(unit % 2 == 1, (view + 1) % VIEWS, VIEWS - 1 - view)
    first = (slot % 2) * 2 + slot // 2
    place = 8 * unit + 2 * slot + core
    numbers = jnp.concatenate(
        [left_views.reshape(-1), right_step.reshape(-1), offset_tile.reshape(-1), place.astype(jnp.int32).reshape(1)]
    )
    row_ids = lax.broadcasted_iota(jnp.int32, (row_count, 1, 1), 0)
    masked = jnp.where(row_ids >= row_count - valid_rows[0], features, jnp.zeros_like(features))
    stays = slot // 2 == core
    pieces = [lax.dynamic_slice_in_dim(masked, 2 * (first ^ m), 2, 0) for m in range(VIEWS)]
    base = [lax.ppermute(pieces[m], "strip", share[m]) for m in range(VIEWS)]
    base[0] = jnp.where(stays, pieces[0], base[0])
    numbers, base = lax.optimization_barrier((numbers, base))
    rows = [jnp.concatenate([lax.dynamic_slice_in_dim(g, r, 1, 0) for g in base], 0) for r in (1 - core, core)]
    beside = lax.ppermute(rows[0], "strip", siblings)
    beyond = lax.ppermute(rows[1], "strip", neighbours)
    done, right, left = band_inner(numbers, base, beside)
    given, right, left = band_given(numbers, beyond, done, right, left, strips)
    taken = lax.ppermute(given, "strip", siblings)
    kept = band_kept(numbers, done, right, left)
    sent = jnp.where(core == 0, jnp.concatenate([kept, taken], 2), jnp.concatenate([taken, kept], 2))
    back = [lax.ppermute(sent[e], "strip", home[e]) for e in range(2)]
    back[1] = jnp.where(stays, sent[1], back[1])
    return jnp.where(slot % 2 == 0, jnp.concatenate(back[::-1], 1), jnp.concatenate(back, 1))


def solution(mesh):
    return jax.shard_map(
        per_device,
        mesh=mesh,
        in_specs=(
            P(("groups", "strip"), None, None),
            P(("groups", "strip")),
            P("groups", None),
            P("groups", None),
            P("groups", None),
        ),
        out_specs=P(None, ("groups", "strip"), None),
        check_vma=False,
    )
```

```python
import functools
import math

import jax
import jax.numpy as jnp
from jax import lax
from jax.experimental import pallas as pl
from jax.experimental.pallas import tpu as pltpu
from jax.sharding import PartitionSpec as P

LEVELS = 256
BX = 128
TILES = 4
VIEWS = 4
ROUNDS = 2
PAIRS = ROUNDS * VIEWS
UNROLL = 4
PAD = (TILES - 1) * BX + LEVELS
SCALE = 0.35 * math.log2(math.e)


def slot_of(view, unit):
    return (view + 1) % VIEWS if unit % 2 else VIEWS - 1 - view


def swap_bits(i):
    return ((i & 1) << 1) | (i >> 1)


def tables(strips):
    per_view = strips // VIEWS

    def device(view, unit, core):
        return (view * per_view + 2 * unit + core + per_view // 2) % strips

    units = per_view // 2
    share = []
    for m in range(VIEWS):
        pairs = []
        for unit in range(units):
            order = sorted(range(VIEWS), key=lambda v: slot_of(v, unit))
            for view in range(VIEWS):
                for core in range(2):
                    slot, here = slot_of(view, unit), device(view, unit, core)
                    place = 4 * core + (swap_bits(slot) ^ m)
                    there = device(order[place // 2], unit, place % 2)
                    pairs.append((here, device(order[slot ^ 1], unit, core) if there == here else there))
        share.append(pairs)
    line = []
    for unit in range(units):
        order = sorted(range(VIEWS), key=lambda v: slot_of(v, unit))
        for place in range(8):
            line.append(device(order[place // 2], unit, place % 2))
    inner = [(line[i], line[i ^ 1]) for i in range(len(line))]
    outer = [(line[i], line[(i + 1) % len(line)]) for i in range(1, len(line), 2)]
    home = []
    for e in range(2):
        pairs = []
        for unit in range(units):
            order = sorted(range(VIEWS), key=lambda v: slot_of(v, unit))
            for view in range(VIEWS):
                for core in range(2):
                    slot = slot_of(view, unit)
                    sender, here = device(order[2 * core + (slot % 2 ^ e ^ 1)], unit, slot // 2), device(view, unit, core)
                    pairs.append((device(order[slot ^ 1], unit, core) if sender == here else sender, here))
        home.append(pairs)
    return share, inner, outer + [(j, i) for i, j in outer], home


def regress(scores, half, x_less_b):
    groups = BX // 8

    def part(span, a):
        first = (span + half) * BX + 8 * a
        return scores[first : first + 8, half * BX : (half + 1) * BX]

    near = [jnp.where(x_less_b < 8 * a, part(0, a), part(2, a)) for a in range(groups)]
    far = [part(1, a) for a in range(groups)]
    tops = [functools.reduce(jnp.maximum, near), functools.reduce(jnp.maximum, far)]
    top = jnp.broadcast_to(jnp.max(jnp.maximum(*tops), axis=0, keepdims=True), (8, BX))

    def weight(value):
        return jnp.exp2((value - top) * SCALE)

    total = moment = weight(far[-1])
    for value in far[-2::-1]:
        total = total + weight(value)
        moment = moment + total
    wrapped = total
    for a in range(groups - 1, -1, -1):
        total = total + weight(near[a])
        wrapped = jnp.where(x_less_b < 8 * a, total, wrapped)
        if a:
            moment = moment + total
    moment = x_less_b.astype(jnp.float32) * total - 8.0 * moment + 256.0 * wrapped
    return jnp.sum(moment, axis=0, keepdims=True) / jnp.sum(total, axis=0, keepdims=True)


class Place:
    def __init__(self, place):
        self.place = place
        self.unit, self.slot, self.core = place // 8, place % 8 // 2, place % 2

    def slot_of(self, view):
        return jnp.where(self.unit % 2 == 1, (view + 1) % VIEWS, VIEWS - 1 - view)

    def view_at(self, slot):
        return jnp.where(self.unit % 2 == 1, (slot + VIEWS - 1) % VIEWS, VIEWS - 1 - slot)

    def view_of(self, buffer):
        return self.view_at(swap_bits((self.place % 4) ^ buffer))

    def buffer_of(self, view):
        return (self.place % 4) ^ swap_bits(self.slot_of(view))

    def view_home(self, group, e):
        return self.view_at(2 * (self.core ^ group) + (e ^ 1 ^ (self.slot % 2)))


def correlate(numbers, at, right, left, result, groups):
    columns = result.shape[-1]
    x_less_b = lax.broadcasted_iota(jnp.int32, (8, BX), 1) - lax.broadcasted_iota(jnp.int32, (8, BX), 0)

    def one_pair(i, carry):
        q, e, group = i % 2, i // 2 % 2, i // 4
        j = VIEWS * q + at.view_home(group, e)
        left_view = numbers[j]
        right_view = (left_view + numbers[PAIRS + j]) % VIEWS
        tile = numbers[2 * PAIRS + j]
        a, b = at.buffer_of(left_view), at.buffer_of(right_view)
        shift = (tile * BX).astype(jnp.float32)
        for n in range(0, columns // BX, 2):
            start = pl.multiple_of((TILES - 1 + n - tile) * BX, BX)
            scores = jnp.dot(
                right[b, pl.ds(start, 2 * BX + LEVELS), :],
                left[a, :, n * BX : (n + 2) * BX],
                preferred_element_type=jnp.float32,
            )
            for k in range(2):
                result[i, :, (n + k) * BX : (n + k + 1) * BX] = regress(scores, k, x_less_b) + shift
        return carry

    lax.fori_loop(4 * groups[0], 4 * groups[-1] + 4, one_pair, 0, unroll=UNROLL)


def shares_of(middle, channels):
    heavy = 0.25 + 0.25 * middle.astype(jnp.float32)
    return [jnp.full((channels, BX), w).astype(jnp.bfloat16) for w in (0.75 - heavy, heavy)]


def band_inner(numbers, kept, base, rim):
    _, channels, columns = base[0].shape
    depth = 4 * channels

    def body(numbers, *refs):
        kept, base, (rim, result, right, outer_left, left) = refs[0], refs[1 : VIEWS + 1], refs[VIEWS + 1 :]
        at = Place(numbers[3 * PAIRS])
        beside = Place(at.place + 1 - 2 * at.core)
        inner, outer = shares_of(1 - at.core, channels), shares_of(at.core, channels)
        nothing = jnp.zeros((channels, BX), jnp.bfloat16)
        for m in range(VIEWS):
            there = beside.buffer_of(at.view_of(m))
            right[m, :PAD, :] = jnp.zeros((PAD, depth), jnp.bfloat16)
            for n in range(columns // BX):
                span = slice(n * BX, (n + 1) * BX)
                pair = [base[m][0, :, span], base[m][1, :, span]]
                if m == 0:
                    pair = [jnp.where(at.slot // 2 == at.core, kept[r, :, span], pair[r]) for r in range(2)]
                third = rim[there, :, span]
                right[m, PAD + n * BX : PAD + (n + 1) * BX, :] = jnp.concatenate([third] + pair + [nothing], 0).T
                mixed = [r * w for r, w in zip(pair, inner)]
                left[m, :, span] = jnp.concatenate([third * jnp.bfloat16(0.25)] + mixed + [nothing], 0)
                mixed = [r * w for r, w in zip(pair, outer)]
                outer_left[m, channels:, span] = jnp.concatenate(mixed + [nothing], 0)
        correlate(numbers, at, right, left, result, (0, 1))

    vmem = pl.BlockSpec(memory_space=pltpu.VMEM)
    return pl.pallas_call(
        body,
        out_shape=[
            jax.ShapeDtypeStruct((PAIRS, 1, columns), jnp.float32),
            jax.ShapeDtypeStruct((VIEWS, PAD + columns, depth), jnp.bfloat16),
            jax.ShapeDtypeStruct((VIEWS, depth, columns), jnp.bfloat16),
        ],
        in_specs=[pl.BlockSpec(memory_space=pltpu.SMEM)] + [vmem] * (VIEWS + 2),
        out_specs=[vmem] * 3,
        scratch_shapes=[pltpu.VMEM((VIEWS, depth, columns), jnp.bfloat16)],
        compiler_params=pltpu.CompilerParams(vmem_limit_bytes=48 << 20),
        name="band_inner",
    )(numbers, kept, *base, rim)


def both_rows(core, first, second, group, out):
    for e in range(2):
        for q in range(ROUNDS):
            i = 4 * group + 2 * e + q
            out[e, q, 0:1, :] = jnp.where(core == 0, first[i], second[i])
            out[e, q, 1:2, :] = jnp.where(core == 0, second[i], first[i])


def band_given(numbers, rim, done, right, left, places):
    _, channels, columns = rim.shape

    def body(numbers, rim, done, right_in, left_in, given, right, left, result):
        at = Place(numbers[3 * PAIRS])
        beyond = Place((at.place - 1 + 2 * at.core + places) % places)
        edge = at.place == jnp.where(at.core == 0, 0, places - 1)
        share = jnp.full((channels, BX), jnp.where(edge, 0.0, 0.25)).astype(jnp.bfloat16)
        for m in range(VIEWS):
            there = beyond.buffer_of(at.view_of(m))
            for n in range(columns // BX):
                span = slice(n * BX, (n + 1) * BX)
                third = rim[there, :, span]
                right[m, PAD + n * BX : PAD + (n + 1) * BX, :channels] = third.T
                left[m, :channels, span] = third * share
        correlate(numbers, at, right, left, result, (1,))
        both_rows(at.core, result, done, 1, given)

    vmem = pl.BlockSpec(memory_space=pltpu.VMEM)
    return pl.pallas_call(
        body,
        out_shape=[
            jax.ShapeDtypeStruct((2, ROUNDS, 2, columns), jnp.float32),
            jax.ShapeDtypeStruct(right.shape, right.dtype),
            jax.ShapeDtypeStruct(left.shape, left.dtype),
        ],
        in_specs=[pl.BlockSpec(memory_space=pltpu.SMEM)] + [vmem] * 4,
        out_specs=[vmem] * 3,
        input_output_aliases={3: 1, 4: 2},
        scratch_shapes=[pltpu.VMEM(done.shape, done.dtype)],
        compiler_params=pltpu.CompilerParams(vmem_limit_bytes=48 << 20),
        name="band_given",
    )(numbers, rim, done, right, left)


def band_kept(numbers, done, right, left):
    columns = done.shape[-1]

    def body(numbers, done, right, left, kept, result):
        at = Place(numbers[3 * PAIRS])
        correlate(numbers, at, right, left, result, (0,))
        both_rows(at.core, result, done, 0, kept)

    vmem = pl.BlockSpec(memory_space=pltpu.VMEM)
    return pl.pallas_call(
        body,
        out_shape=jax.ShapeDtypeStruct((2, ROUNDS, 2, columns), jnp.float32),
        in_specs=[pl.BlockSpec(memory_space=pltpu.SMEM)] + [vmem] * 3,
        out_specs=vmem,
        scratch_shapes=[pltpu.VMEM(done.shape, done.dtype)],
        compiler_params=pltpu.CompilerParams(vmem_limit_bytes=48 << 20),
        name="band_kept",
    )(numbers, done, right, left)


def per_device(features, valid_rows, left_views, right_step, offset_tile):
    row_count = features.shape[0]
    strips = lax.axis_size("strip")
    per_view = strips // VIEWS
    share, siblings, neighbours, home = tables(strips)
    index = (lax.axis_index("strip") - per_view // 2) % strips
    view, spot = index // per_view, index % per_view
    unit, core = spot // 2, spot % 2
    slot = jnp.where(unit % 2 == 1, (view + 1) % VIEWS, VIEWS - 1 - view)
    first = ((slot % 2) * 2 + slot // 2)
    place = 8 * unit + 2 * slot + core
    numbers = jnp.concatenate(
        [left_views.reshape(-1), right_step.reshape(-1), offset_tile.reshape(-1), place.astype(jnp.int32).reshape(1)]
    )
    row_ids = lax.broadcasted_iota(jnp.int32, (row_count, 1, 1), 0)
    masked = jnp.where(row_ids >= row_count - valid_rows[0], features, jnp.zeros_like(features))
    stays = slot // 2 == core
    pieces = [lax.dynamic_slice_in_dim(masked, 2 * (first ^ m), 2, 0) for m in range(VIEWS)]
    base = [lax.ppermute(pieces[m], "strip", share[m]) for m in range(VIEWS)]
    numbers, base = lax.optimization_barrier((numbers, base))
    whole = list(base)
    whole[0] = jnp.where(stays, pieces[0], base[0])
    rows = [jnp.concatenate([lax.dynamic_slice_in_dim(g, r, 1, 0) for g in whole], 0) for r in (1 - core, core)]
    beside = lax.ppermute(rows[0], "strip", siblings)
    beyond = lax.ppermute(rows[1], "strip", neighbours)
    done, right, left = band_inner(numbers, pieces[0], base, beside)
    given, right, left = band_given(numbers, beyond, done, right, left, strips)
    taken = lax.ppermute(given, "strip", siblings)
    kept = band_kept(numbers, done, right, left)
    sent = jnp.where(core == 0, jnp.concatenate([kept, taken], 2), jnp.concatenate([taken, kept], 2))
    back = [lax.ppermute(sent[e], "strip", home[e]) for e in range(2)]
    back[1] = jnp.where(stays, sent[1], back[1])
    return jnp.where(slot % 2 == 0, jnp.concatenate(back[::-1], 1), jnp.concatenate(back, 1))


def solution(mesh):
    return jax.shard_map(
        per_device,
        mesh=mesh,
        in_specs=(
            P(("groups", "strip"), None, None),
            P(("groups", "strip")),
            P("groups", None),
            P("groups", None),
            P("groups", None),
        ),
        out_specs=P(None, ("groups", "strip"), None),
        check_vma=False,
    )
```

```python
import functools
import math

import jax
import jax.numpy as jnp
from jax import lax
from jax.experimental import pallas as pl
from jax.experimental.pallas import tpu as pltpu
from jax.sharding import PartitionSpec as P

LEVELS = 256
BX = 128
TILES = 4
VIEWS = 4
ROUNDS = 2
PAIRS = ROUNDS * VIEWS
UNROLL = 4
PAD = (TILES - 1) * BX + LEVELS
SCALE = 0.35 * math.log2(math.e)


def slot_of(view, unit):
    return (view + 1) % VIEWS if unit % 2 else VIEWS - 1 - view


def swap_bits(i):
    return ((i & 1) << 1) | (i >> 1)


def tables(strips):
    per_view = strips // VIEWS

    def device(view, unit, core):
        return (view * per_view + 2 * unit + core + per_view // 2) % strips

    units = per_view // 2
    share = []
    for m in range(VIEWS):
        pairs = []
        for unit in range(units):
            order = sorted(range(VIEWS), key=lambda v: slot_of(v, unit))
            for view in range(VIEWS):
                for core in range(2):
                    slot, here = slot_of(view, unit), device(view, unit, core)
                    place = 4 * core + (swap_bits(slot) ^ m)
                    there = device(order[place // 2], unit, place % 2)
                    pairs.append((here, device(order[slot ^ 1], unit, core) if there == here else there))
        share.append(pairs)
    line = []
    for unit in range(units):
        order = sorted(range(VIEWS), key=lambda v: slot_of(v, unit))
        for place in range(8):
            line.append(device(order[place // 2], unit, place % 2))
    inner = [(line[i], line[i ^ 1]) for i in range(len(line))]
    outer = [(line[i], line[(i + 1) % len(line)]) for i in range(1, len(line), 2)]
    home = []
    for e in range(2):
        pairs = []
        for unit in range(units):
            order = sorted(range(VIEWS), key=lambda v: slot_of(v, unit))
            for view in range(VIEWS):
                for core in range(2):
                    slot = slot_of(view, unit)
                    sender, here = device(order[2 * core + (slot % 2 ^ e ^ 1)], unit, slot // 2), device(view, unit, core)
                    pairs.append((device(order[slot ^ 1], unit, core) if sender == here else sender, here))
        home.append(pairs)
    return share, inner, outer + [(j, i) for i, j in outer], home


def regress(scores, half, x_less_b):
    groups = BX // 8

    def part(span, a):
        first = (span + half) % 2 * BX + 8 * a
        return scores[(span + half) // 2][first : first + 8, half * BX : (half + 1) * BX]

    near = [jnp.where(x_less_b < 8 * a, part(0, a), part(2, a)) for a in range(groups)]
    far = [part(1, a) for a in range(groups)]
    tops = [functools.reduce(jnp.maximum, near), functools.reduce(jnp.maximum, far)]
    top = jnp.broadcast_to(jnp.max(jnp.maximum(*tops), axis=0, keepdims=True), (8, BX))

    def weight(value):
        return jnp.exp2((value - top) * SCALE)

    total = moment = weight(far[-1])
    for value in far[-2::-1]:
        total = total + weight(value)
        moment = moment + total
    wrapped = total
    for a in range(groups - 1, -1, -1):
        total = total + weight(near[a])
        wrapped = jnp.where(x_less_b < 8 * a, total, wrapped)
        if a:
            moment = moment + total
    moment = x_less_b.astype(jnp.float32) * total - 8.0 * moment + 256.0 * wrapped
    return jnp.sum(moment, axis=0, keepdims=True) / jnp.sum(total, axis=0, keepdims=True)


class Place:
    def __init__(self, place):
        self.place = place
        self.unit, self.slot, self.core = place >> 3, (place >> 1) & 3, place & 1

    def slot_of(self, view):
        return jnp.where((self.unit & 1) == 1, (view + 1) & (VIEWS - 1), VIEWS - 1 - view)

    def view_at(self, slot):
        return jnp.where((self.unit & 1) == 1, (slot + VIEWS - 1) & (VIEWS - 1), VIEWS - 1 - slot)

    def view_of(self, buffer):
        return self.view_at(swap_bits((self.place & 3) ^ buffer))

    def buffer_of(self, view):
        return (self.place & 3) ^ swap_bits(self.slot_of(view))

    def view_home(self, group, e):
        return self.view_at(2 * (self.core ^ group) + (e ^ 1 ^ (self.slot & 1)))


def correlate(numbers, at, right, left, result, groups):
    columns = result.shape[-1]
    x_less_b = lax.broadcasted_iota(jnp.int32, (8, BX), 1) - lax.broadcasted_iota(jnp.int32, (8, BX), 0)

    def one_pair(i, carry):
        q, e, group = i & 1, (i >> 1) & 1, i >> 2
        j = VIEWS * q + at.view_home(group, e)
        left_view = numbers[j]
        right_view = (left_view + numbers[PAIRS + j]) & (VIEWS - 1)
        tile = numbers[2 * PAIRS + j]
        a, b = at.buffer_of(left_view), at.buffer_of(right_view)
        shift = (tile * BX).astype(jnp.float32)
        for n in range(0, columns // BX, 2):
            start = pl.multiple_of((TILES - 1 + n - tile) * BX, BX)
            scores = [
                jnp.dot(
                    right[b, pl.ds(start + i * 2 * BX, 2 * BX), :],
                    left[a, :, n * BX : (n + 2) * BX],
                    preferred_element_type=jnp.float32,
                )
                for i in range(2)
            ]
            for k in range(2):
                result[i, :, (n + k) * BX : (n + k + 1) * BX] = regress(scores, k, x_less_b) + shift
        return carry

    lax.fori_loop(4 * groups[0], 4 * groups[-1] + 4, one_pair, 0, unroll=UNROLL)


def shares_of(middle, channels):
    heavy = 0.25 + 0.25 * middle.astype(jnp.float32)
    return [jnp.full((channels, BX), w).astype(jnp.bfloat16) for w in (0.75 - heavy, heavy)]


def band_inner(numbers, kept, base, rim):
    _, channels, columns = base[0].shape
    depth = 4 * channels

    def body(numbers, *refs):
        kept, base, (rim, result, right, outer_left, left) = refs[0], refs[1 : VIEWS + 1], refs[VIEWS + 1 :]
        at = Place(numbers[3 * PAIRS])
        beside = Place(at.place + 1 - 2 * at.core)
        inner, outer = shares_of(1 - at.core, channels), shares_of(at.core, channels)
        nothing = jnp.zeros((channels, BX), jnp.bfloat16)
        for m in range(VIEWS):
            there = beside.buffer_of(at.view_of(m))
            right[m, :PAD, :] = jnp.zeros((PAD, depth), jnp.bfloat16)
            for n in range(columns // BX):
                span = slice(n * BX, (n + 1) * BX)
                pair = [base[m][0, :, span], base[m][1, :, span]]
                if m == 0:
                    pair = [jnp.where((at.slot >> 1) == at.core, kept[r, :, span], pair[r]) for r in range(2)]
                third = rim[there, :, span]
                right[m, PAD + n * BX : PAD + (n + 1) * BX, :] = jnp.concatenate([third] + pair + [nothing], 0).T
                mixed = [r * w for r, w in zip(pair, inner)]
                left[m, :, span] = jnp.concatenate([third * jnp.bfloat16(0.25)] + mixed + [nothing], 0)
                mixed = [r * w for r, w in zip(pair, outer)]
                outer_left[m, channels:, span] = jnp.concatenate(mixed + [nothing], 0)
        correlate(numbers, at, right, left, result, (0, 1))

    vmem = pl.BlockSpec(memory_space=pltpu.VMEM)
    return pl.pallas_call(
        body,
        out_shape=[
            jax.ShapeDtypeStruct((PAIRS, 1, columns), jnp.float32),
            jax.ShapeDtypeStruct((VIEWS, PAD + columns, depth), jnp.bfloat16),
            jax.ShapeDtypeStruct((VIEWS, depth, columns), jnp.bfloat16),
        ],
        in_specs=[pl.BlockSpec(memory_space=pltpu.SMEM)] + [vmem] * (VIEWS + 2),
        out_specs=[vmem] * 3,
        scratch_shapes=[pltpu.VMEM((VIEWS, depth, columns), jnp.bfloat16)],
        compiler_params=pltpu.CompilerParams(vmem_limit_bytes=48 << 20),
        name="band_inner",
    )(numbers, kept, *base, rim)


def both_rows(core, first, second, group, out):
    for e in range(2):
        for q in range(ROUNDS):
            i = 4 * group + 2 * e + q
            out[e, q, 0:1, :] = jnp.where(core == 0, first[i], second[i])
            out[e, q, 1:2, :] = jnp.where(core == 0, second[i], first[i])


def band_given(numbers, rim, done, right, left, places):
    _, channels, columns = rim.shape

    def body(numbers, rim, done, right_in, left_in, given, right, left, result):
        at = Place(numbers[3 * PAIRS])
        neighbour = at.place - 1 + 2 * at.core
        beyond = Place(jnp.where(neighbour < 0, places - 1, jnp.where(neighbour == places, 0, neighbour)))
        edge = at.place == jnp.where(at.core == 0, 0, places - 1)
        share = jnp.full((channels, BX), jnp.where(edge, 0.0, 0.25)).astype(jnp.bfloat16)
        for m in range(VIEWS):
            there = beyond.buffer_of(at.view_of(m))
            for n in range(columns // BX):
                span = slice(n * BX, (n + 1) * BX)
                third = rim[there, :, span]
                right[m, PAD + n * BX : PAD + (n + 1) * BX, :channels] = third.T
                left[m, :channels, span] = third * share
        correlate(numbers, at, right, left, result, (1,))
        both_rows(at.core, result, done, 1, given)

    vmem = pl.BlockSpec(memory_space=pltpu.VMEM)
    return pl.pallas_call(
        body,
        out_shape=[
            jax.ShapeDtypeStruct((2, ROUNDS, 2, columns), jnp.float32),
            jax.ShapeDtypeStruct(right.shape, right.dtype),
            jax.ShapeDtypeStruct(left.shape, left.dtype),
        ],
        in_specs=[pl.BlockSpec(memory_space=pltpu.SMEM)] + [vmem] * 4,
        out_specs=[vmem] * 3,
        input_output_aliases={3: 1, 4: 2},
        scratch_shapes=[pltpu.VMEM(done.shape, done.dtype)],
        compiler_params=pltpu.CompilerParams(vmem_limit_bytes=48 << 20),
        name="band_given",
    )(numbers, rim, done, right, left)


def band_kept(numbers, done, right, left):
    columns = done.shape[-1]

    def body(numbers, done, right, left, kept, result):
        at = Place(numbers[3 * PAIRS])
        correlate(numbers, at, right, left, result, (0,))
        both_rows(at.core, result, done, 0, kept)

    vmem = pl.BlockSpec(memory_space=pltpu.VMEM)
    return pl.pallas_call(
        body,
        out_shape=jax.ShapeDtypeStruct((2, ROUNDS, 2, columns), jnp.float32),
        in_specs=[pl.BlockSpec(memory_space=pltpu.SMEM)] + [vmem] * 3,
        out_specs=vmem,
        scratch_shapes=[pltpu.VMEM(done.shape, done.dtype)],
        compiler_params=pltpu.CompilerParams(vmem_limit_bytes=48 << 20),
        name="band_kept",
    )(numbers, done, right, left)


def per_device(features, valid_rows, left_views, right_step, offset_tile):
    row_count = features.shape[0]
    strips = lax.axis_size("strip")
    per_view = strips // VIEWS
    share, siblings, neighbours, home = tables(strips)
    index = (lax.axis_index("strip") - per_view // 2) % strips
    view, spot = index // per_view, index % per_view
    unit, core = spot // 2, spot % 2
    slot = jnp.where(unit % 2 == 1, (view + 1) % VIEWS, VIEWS - 1 - view)
    first = ((slot % 2) * 2 + slot // 2)
    place = 8 * unit + 2 * slot + core
    numbers = jnp.concatenate(
        [left_views.reshape(-1), right_step.reshape(-1), offset_tile.reshape(-1), place.astype(jnp.int32).reshape(1)]
    )
    row_ids = lax.broadcasted_iota(jnp.int32, (row_count, 1, 1), 0)
    masked = jnp.where(row_ids >= row_count - valid_rows[0], features, jnp.zeros_like(features))
    stays = slot // 2 == core
    pieces = [lax.dynamic_slice_in_dim(masked, 2 * (first ^ m), 2, 0) for m in range(VIEWS)]
    base = [lax.ppermute(pieces[m], "strip", share[m]) for m in range(VIEWS)]
    numbers, base = lax.optimization_barrier((numbers, base))
    whole = list(base)
    whole[0] = jnp.where(stays, pieces[0], base[0])
    rows = [jnp.concatenate([lax.dynamic_slice_in_dim(g, r, 1, 0) for g in whole], 0) for r in (1 - core, core)]
    beside = lax.ppermute(rows[0], "strip", siblings)
    beyond = lax.ppermute(rows[1], "strip", neighbours)
    done, right, left = band_inner(numbers, pieces[0], base, beside)
    given, right, left = band_given(numbers, beyond, done, right, left, strips)
    taken = lax.ppermute(given, "strip", siblings)
    kept = band_kept(numbers, done, right, left)
    sent = jnp.where(core == 0, jnp.concatenate([kept, taken], 2), jnp.concatenate([taken, kept], 2))
    back = [lax.ppermute(sent[e], "strip", home[e]) for e in range(2)]
    back[1] = jnp.where(stays, sent[1], back[1])
    return jnp.where(slot % 2 == 0, jnp.concatenate(back[::-1], 1), jnp.concatenate(back, 1))


def solution(mesh):
    return jax.shard_map(
        per_device,
        mesh=mesh,
        in_specs=(
            P(("groups", "strip"), None, None),
            P(("groups", "strip")),
            P("groups", None),
            P("groups", None),
            P("groups", None),
        ),
        out_specs=P(None, ("groups", "strip"), None),
        check_vma=False,
    )
```
